256 devices in a mesh: row: 8 (over x, y_hi), col: 16 (over y_lo, z), layer: 2 (over core).
Axes of the slice: x: 4, y: 4 (y_hi: 2, y_lo: 2; y = y_hi * 2 + y_lo), z: 8, core: 2. Of those that a mesh axis runs over, the one named last changes fastest.
Arguments:
- upper: float32 [1536, 7, 128, 128], P(('row', 'col')), may hold values from -2.5 to 2.5
- block_mask: int32 [1536, 7], P(('row', 'col')), may hold values 0 or 1
- keep_mask: int32 [1536, 13], P(('row', 'col')), may hold values 0 or 1
Outputs:
- product: float32 [1536, 13, 128, 128], P(('row', 'col'), None, 'layer')
The draws below stay inside these ranges and needn't reach their ends.
All inputs are finite; a program needn't handle non-finite values. No bound on the sum of `block_mask` or of `keep_mask` on one device may be relied on, other than what follows from the above.
Results may differ from the reference program's by a relative error of at most 0.0001.
Values sent between devices are 32-bit elements; how exact they have to be, the bound alone decides.
A program may use at most 128 MiB of HBM per device.

```python
import jax
import jax.numpy as jnp
from jax import lax

B = 128
H = 6
NB = 1536


def touch_ends(values, rng, low, top_value):
    longest = values.shape.index(max(values.shape))
    spots = []
    for shift in (0, 1):
        where = [jax.random.randint(jax.random.fold_in(rng, axis), (), 0, length) for axis, length in enumerate(values.shape)]
        where[longest] = (where[longest] + shift) % values.shape[longest]
        spots.append(tuple(where))
    return values.at[spots[0]].set(low).at[spots[1]].set(top_value)


def block_scale(stream_key, shape, split, smallest, high):
    factor_of = 1.0
    for dim, parts in split:
        heights = jax.random.uniform(jax.random.fold_in(jax.random.fold_in(stream_key, 6), dim), (parts,), jnp.float32, smallest / len(split), high / len(split))
        factor_of = factor_of * jnp.repeat(jnp.exp(heights), shape[dim] // parts).reshape((-1,) + (1,) * (len(shape) - 1 - dim))
    return factor_of


def bell_draw(own_key, extent, scale, bound, shards=(), held_as=jnp.bfloat16):
    entries = jax.random.normal(own_key, extent, jnp.float32) * scale
    if len(shards) > 0:
        entries = block_scale(own_key, extent, shards, -0.22, 0.18) * entries
    return jnp.clip(entries, min=-bound, max=bound).astype(held_as)


def setup_inputs(seed: int = 0) -> dict:
    key_of = jax.random.split(jax.random.key(seed), 4)
    upper = bell_draw(key_of[0], (NB, H + 1, B, B), 0.16, 2.5, ((0, 128),), jnp.float32)
    block_mask = touch_ends((jax.random.randint(key_of[1], (NB, H + 1), 0, 4) < 3).astype(jnp.int32), jax.random.fold_in(key_of[1], 1), 0, 1)
    keep_mask = touch_ends((jax.random.randint(key_of[2], (NB, 2 * H + 1), 0, 3) < 2).astype(jnp.int32), jax.random.fold_in(key_of[2], 1), 0, 1)
    return {"upper": upper, "block_mask": block_mask, "keep_mask": keep_mask}


def prepare(upper, block_mask, first_row, total_rows):
    row_count, width = block_mask.shape
    global_row = first_row + lax.broadcasted_iota(jnp.int32, (row_count, width), 0)
    offset_k = lax.broadcasted_iota(jnp.int32, (row_count, width), 1)
    present = ((block_mask == 1) | (offset_k == 0)) & (global_row + offset_k < total_rows)
    weights = jnp.where(present, jnp.float32(1.0), jnp.float32(0.0)).astype(jnp.float32)
    stored = upper * weights[:, :, None, None]
    diagonal = stored[:, 0]
    diagonal = 0.5 * (diagonal + jnp.swapaxes(diagonal, 1, 2))
    return jnp.concatenate([diagonal[:, None], stored[:, 1:]], axis=1)


def right_block(window, band_reach, offset, column):
    gap = column - offset
    if gap >= 0:
        return window[band_reach + offset, gap]
    return jnp.swapaxes(window[band_reach + column, -gap], 0, 1)


def block_row(window, band_reach, cut_left):
    left_blocks = []
    for offset in range(-band_reach, band_reach + 1):
        if offset >= 0:
            left_blocks.append(window[band_reach, offset])
        else:
            left_blocks.append(jnp.swapaxes(window[band_reach + offset, -offset], 0, 1))
    results = []
    for column in range(2 * band_reach + 1):
        left_stack = cut_left(jnp.stack(left_blocks[column:]))
        right_stack = jnp.stack([right_block(window, band_reach, offset, column) for offset in range(column - band_reach, band_reach + 1)])
        results.append(jnp.einsum("tab,tbc->ac", left_stack, right_stack, precision=lax.Precision.HIGHEST))
    return jnp.stack(results)


def unchanged(stack):
    return stack


def reference(upper, block_mask, keep_mask):
    total_rows = upper.shape[0]
    band_reach = upper.shape[1] - 1
    block_size = upper.shape[2]
    stored = prepare(upper, block_mask, 0, total_rows)
    before = jnp.zeros((band_reach, band_reach + 1, block_size, block_size), jnp.float32)
    after = jnp.zeros((band_reach, band_reach + 1, block_size, block_size), jnp.float32)
    padded = jnp.concatenate([before, stored, after], axis=0)

    def one_row(row_at):
        window = lax.dynamic_slice_in_dim(padded, row_at, 2 * band_reach + 1, 0)
        return block_row(window, band_reach, unchanged)

    product = lax.map(one_row, jnp.arange(total_rows, dtype=jnp.int32))
    global_row = lax.broadcasted_iota(jnp.int32, keep_mask.shape, 0)
    column_m = lax.broadcasted_iota(jnp.int32, keep_mask.shape, 1)
    kept = jnp.where((keep_mask == 1) & (global_row + column_m < total_rows), jnp.float32(1.0), jnp.float32(0.0)).astype(jnp.float32)
    return product * kept[:, :, None, None]
```

```python
import functools

import jax
import jax.numpy as jnp
from jax import lax
from jax.experimental import pallas as pl
from jax.experimental.pallas import tpu as pltpu
from jax.sharding import PartitionSpec as P

MESH = pl.DeviceIdType.MESH
B = 128
H = 6
ROWS = 12
PAIRS = ROWS // 2
WINDOW = 2 * H + 2
HALF = B // 2


def masked(weight, block):
    return block * weight


def split(x):
    hi = x.astype(jnp.bfloat16)
    lo = (x - hi.astype(jnp.float32)).astype(jnp.bfloat16)
    return hi, lo


def kernel(
    up, mask_s, mask_v, keep_s, out,
    own, behind, ahead, mask_b, mask_a, right_hi, right_lo, left,
    load_sem, send_sem, recv_sem, pass_send, pass_recv, mask_send, mask_recv, ready,
):
    row, col, layer = lax.axis_index("row"), lax.axis_index("col"), lax.axis_index("layer")
    n_col = lax.axis_size("col")
    n_part = lax.axis_size("row") * n_col
    total_rows = n_part * ROWS
    part = row * n_col + col
    after = lax.rem(part + 1, n_part)
    before = lax.rem(part + n_part - 1, n_part)
    nxt = (after // n_col, lax.rem(after, n_col), layer)
    prv = (before // n_col, lax.rem(before, n_col), layer)
    sib = (row, col, 1 - layer)
    first_row = part * ROWS
    half = pl.ds(pl.multiple_of(layer * HALF, HALF), HALF)

    def head(j):
        return pltpu.make_async_remote_copy(
            src_ref=up.at[j, :, half, :], dst_ref=ahead.at[j, :, half, :],
            send_sem=send_sem.at[j], recv_sem=recv_sem.at[j], device_id=prv, device_id_type=MESH)

    def tail(a):
        return pltpu.make_async_remote_copy(
            src_ref=up.at[ROWS - 1 - a, pl.ds(a + 1, H - a), half, :],
            dst_ref=behind.at[a, pl.ds(0, H - a), half, :],
            send_sem=send_sem.at[H + a], recv_sem=recv_sem.at[H + a], device_id=nxt, device_id_type=MESH)

    def head_pass(j):
        return pltpu.make_async_remote_copy(
            src_ref=ahead.at[j, :, half, :], dst_ref=ahead.at[j, :, half, :],
            send_sem=pass_send.at[j], recv_sem=pass_recv.at[j], device_id=sib, device_id_type=MESH)

    def tail_pass(a):
        return pltpu.make_async_remote_copy(
            src_ref=behind.at[a, pl.ds(0, H - a), half, :], dst_ref=behind.at[a, pl.ds(0, H - a), half, :],
            send_sem=pass_send.at[H + a], recv_sem=pass_recv.at[H + a], device_id=sib, device_id_type=MESH)

    mask_head = pltpu.make_async_remote_copy(
        src_ref=mask_v, dst_ref=mask_a, send_sem=mask_send.at[0], recv_sem=mask_recv.at[0],
        device_id=prv, device_id_type=MESH)
    mask_tail = pltpu.make_async_remote_copy(
        src_ref=mask_v, dst_ref=mask_b, send_sem=mask_send.at[1], recv_sem=mask_recv.at[1],
        device_id=nxt, device_id_type=MESH)
    load = pltpu.make_async_copy(up, own, load_sem)

    barrier = pltpu.get_barrier_semaphore()
    pl.semaphore_signal(barrier, inc=1, device_id=nxt, device_id_type=MESH)
    pl.semaphore_signal(barrier, inc=1, device_id=sib, device_id_type=MESH)
    load.start()
    pl.semaphore_wait(barrier, 2)
    mask_head.start()
    for j in range(H):
        head(j).start()
    pl.semaphore_signal(ready, inc=1, device_id=prv, device_id_type=MESH)

    zero_right = jnp.zeros((B, B), jnp.bfloat16)
    zero_left = jnp.zeros((HALF, B), jnp.bfloat16)

    def clear(pair, carry):
        for ref in (right_hi, right_lo):
            ref[pair, pl.ds(0, B), pl.ds(B, B)] = zero_right
            ref[pair, pl.ds((WINDOW - 1) * B, B), pl.ds(0, B)] = zero_right
        return carry

    lax.fori_loop(0, 2 * PAIRS, clear, 0)

    def clear_left(pair, carry):
        for base in (0, B):
            left[pair, pl.ds(base, HALF), pl.ds((WINDOW - 1) * B, B)] = zero_left
            left[pair, pl.ds(base + HALF, HALF), pl.ds(0, B)] = zero_left
        return carry

    lax.fori_loop(0, PAIRS, clear_left, 0)

    pl.semaphore_wait(ready, 1)
    mask_tail.start()
    for a in range(H):
        tail(a).start()
    load.wait()

    def place_right(pair, r, k, x):
        hi, lo = split(x)
        at = pair + (r + k) // 2
        rows = pl.ds((r + H - 2 * ((r + k) // 2)) * B, B)
        lanes = pl.ds(((r + k) % 2) * B, B)
        right_hi[at, rows, lanes] = hi
        right_lo[at, rows, lanes] = lo

    def place_right_t(pair, r, k, xt):
        hi, lo = split(xt)
        rows = pl.ds((r + k + H) * B, B)
        right_hi[pair, rows, pl.ds(r * B, B)] = hi
        right_lo[pair, rows, pl.ds(r * B, B)] = lo

    def my_half(x):
        return jnp.where(layer == 0, x[:HALF], x[HALF:])

    def place_left(pair, r, offset, xh):
        hi, lo = split(xh)
        lanes = pl.ds((r + offset + H) * B, B)
        left[pair, pl.ds(r * HALF, HALF), lanes] = hi
        left[pair, pl.ds(B + r * HALF, HALF), lanes] = lo

    def own_pair(pair, carry):
        for r in range(2):
            for k in range(H + 1):
                j = 2 * pair + r
                inside = first_row + j + k < total_rows
                if k > 0:
                    inside = inside & (mask_s[j, k] == 1)
                weight = jnp.where(inside, jnp.float32(1.0), jnp.float32(0.0))
                x = masked(weight, own[j, k])
                xt = x.T
                if k == 0:
                    x = 0.5 * (x + xt)
                place_right(pair, r, k, x)
                place_left(pair, r, k, my_half(x))
                if k > 0:
                    place_right_t(pair, r, k, xt)
                    own_row = pair + (r + k) // 2

                    @pl.when(own_row < PAIRS)
                    def _():
                        place_left(own_row, (r + k) % 2, -k, my_half(xt))

        return carry

    lax.fori_loop(0, PAIRS, own_pair, 0)

    def multiply(pair, d, lo_block, hi_block):
        n = (hi_block - lo_block) * B
        lanes = pl.ds((2 * d + lo_block) * B, n)
        rows = pl.ds(lo_block * B, n)
        both = jnp.dot(left[pair, :, lanes], right_hi[pair + d, rows, :], preferred_element_type=jnp.float32)
        rest = jnp.dot(left[pair, pl.ds(0, B), lanes], right_lo[pair + d, rows, :], preferred_element_type=jnp.float32)
        return both[:B] + (both[B:] + rest)

    def emit(pair, d, total, add):
        for r in range(2):
            for s in range(2):
                m = 2 * d + s - r
                if 0 <= m <= 2 * H:
                    i = 2 * pair + r
                    kept = (keep_s[i, m] == 1) & (first_row + i + m < total_rows)
                    weight = jnp.where(kept, jnp.float32(1.0), jnp.float32(0.0))
                    piece = total[r * HALF : (r + 1) * HALF, s * B : (s + 1) * B] * weight
                    if add:
                        out[i, m] += piece
                    else:
                        out[i, m] = piece

    def own_low(d, first):
        def body(pair, carry):
            emit(pair, d, multiply(pair, d, 0, WINDOW - 2 * d), False)
            return carry

        lax.fori_loop(first, H // 2, body, 0)

    for d in range(H + 1):
        own_low(d, max(0, H // 2 - d))
    for pair in range(H // 2, PAIRS):
        for d in range(H + 1):
            c = pair + d
            if c < PAIRS:
                emit(pair, d, multiply(pair, d, 0, WINDOW - 2 * d), False)
            elif c < PAIRS + H // 2:
                emit(pair, d, multiply(pair, d, 0, 2 * (PAIRS + H // 2 - c)), False)

    for a in range(H):
        tail(a).wait_recv()
        tail_pass(a).start()
    mask_tail.wait_recv()
    for a in range(H):
        tail_pass(a).wait_recv()
        j = -1 - a
        pair, r = j // 2, j % 2
        for k in range(a + 1, H + 1):
            present = (mask_b[pl.ds(ROWS + j, 1), pl.ds(k, 1)] == 1) & (part > 0)
            x = masked(jnp.where(present, jnp.float32(1.0), jnp.float32(0.0)), behind[a, k - a - 1])
            place_right(pair, r, k, x)
            place_left(pair + (r + k) // 2, (r + k) % 2, -k, my_half(x.T))
    for pair in range(H // 2):
        for d in range(H // 2 - pair):
            emit(pair, d, multiply(pair, d, 0, WINDOW - 2 * d), False)

    mask_head.wait_recv()
    for q in range(H // 2):
        for r in range(2):
            head(2 * q + r).wait_recv()
            head_pass(2 * q + r).start()
        for r in range(2):
            j = 2 * q + r
            head_pass(j).wait_recv()
            for k in range(H + 1):
                present = first_row + ROWS + j + k < total_rows
                weight = jnp.where(present, jnp.float32(1.0), jnp.float32(0.0))
                if k > 0:
                    weight = jnp.where(mask_a[pl.ds(j, 1), pl.ds(k, 1)] == 1, weight, jnp.float32(0.0))
                x = masked(weight, ahead[j, k])
                if k == 0:
                    x = 0.5 * (x + x.T)
                place_right(PAIRS + q, r, k, x)
                if 0 < k < H - j:
                    place_right_t(PAIRS + q, r, k, x.T)
        for pair in range(H // 2 + q, PAIRS):
            for c in range(PAIRS, PAIRS + q + H // 2 + 1):
                d = c - pair
                at = 2 * (PAIRS + q - (c - H // 2))
                first = c >= PAIRS + H // 2 and q == c - PAIRS - H // 2
                emit(pair, d, multiply(pair, d, at, at + 2), not first)

    for j in range(H):
        head(j).wait_send()
        tail(j).wait_send()
        head_pass(j).wait_send()
        tail_pass(j).wait_send()
    mask_head.wait_send()
    mask_tail.wait_send()


def on_device(upper, block_mask, keep_mask):
    f32, bf16 = jnp.float32, jnp.bfloat16
    window = WINDOW * B
    return pl.pallas_call(
        kernel,
        out_shape=jax.ShapeDtypeStruct((ROWS, 2 * H + 1, HALF, B), f32),
        in_specs=[
            pl.BlockSpec(memory_space=pltpu.HBM),
            pl.BlockSpec(memory_space=pltpu.SMEM),
            pl.BlockSpec(memory_space=pltpu.VMEM),
            pl.BlockSpec(memory_space=pltpu.SMEM),
        ],
        out_specs=pl.BlockSpec(memory_space=pltpu.VMEM),
        scratch_shapes=[
            pltpu.VMEM((ROWS, H + 1, B, B), f32),
            pltpu.VMEM((H, H, B, B), f32),
            pltpu.VMEM((H, H + 1, B, B), f32),
            pltpu.VMEM(block_mask.shape, jnp.int32),
            pltpu.VMEM(block_mask.shape, jnp.int32),
            pltpu.VMEM((2 * PAIRS, window, 2 * B), bf16),
            pltpu.VMEM((2 * PAIRS, window, 2 * B), bf16),
            pltpu.VMEM((PAIRS, 2 * B, window), bf16),
            pltpu.SemaphoreType.DMA,
            pltpu.SemaphoreType.DMA((2 * H,)),
            pltpu.SemaphoreType.DMA((2 * H,)),
            pltpu.SemaphoreType.DMA((2 * H,)),
            pltpu.SemaphoreType.DMA((2 * H,)),
            pltpu.SemaphoreType.DMA((2,)),
            pltpu.SemaphoreType.DMA((2,)),
            pltpu.SemaphoreType.REGULAR,
        ],
        compiler_params=pltpu.CompilerParams(
            collective_id=0, has_side_effects=True, vmem_limit_bytes=56 * 2**20
        ),
    )(upper, block_mask, block_mask, keep_mask)


def solution(mesh):
    in_specs = (
        P(("row", "col"), None, None, None),
        P(("row", "col"), None),
        P(("row", "col"), None),
    )
    out_specs = P(("row", "col"), None, "layer", None)
    return jax.shard_map(
        on_device, mesh=mesh, in_specs=in_specs, out_specs=out_specs, check_vma=False
    )
```

```python
import functools

import jax
import jax.numpy as jnp
from jax import lax
from jax.experimental import pallas as pl
from jax.experimental.pallas import tpu as pltpu
from jax.sharding import PartitionSpec as P

MESH = pl.DeviceIdType.MESH
B = 128
H = 6
ROWS = 12
PAIRS = ROWS // 2
WINDOW = 2 * H + 2
HALF = B // 2


def masked(weight, block):
    return block * weight


def split(x):
    hi = x.astype(jnp.bfloat16)
    lo = (x - hi.astype(jnp.float32)).astype(jnp.bfloat16)
    return hi, lo


def window_product(left, right_hi, right_lo, pair, d, lo_block, hi_block):
    n = (hi_block - lo_block) * B
    lanes = pl.ds((2 * d + lo_block) * B, n)
    rows = pl.ds(lo_block * B, n)
    both = jnp.dot(left[pair, :, lanes], right_hi[pair + d, rows, :], preferred_element_type=jnp.float32)
    rest = jnp.dot(left[pair, pl.ds(0, B), lanes], right_lo[pair + d, rows, :], preferred_element_type=jnp.float32)
    return both[:B] + (both[B:] + rest)


def places(d):
    spots = [(r, s, 2 * d + s - r) for r in range(2) for s in range(2)]
    return [spot for spot in spots if 0 <= spot[2] <= 2 * H]


def quarter(total, r, s):
    return total[r * HALF : (r + 1) * HALF, s * B : (s + 1) * B]


def keep_weight(keep_s, i, m, first_row, total_rows):
    kept = (keep_s[i, m] == 1) & (first_row + i + m < total_rows)
    return jnp.where(kept, jnp.float32(1.0), jnp.float32(0.0))


def finish(out, right_hi, right_lo, left, keep_s, final, tail, sem):
    n_part = lax.axis_size("row") * lax.axis_size("col")
    first_row = (lax.axis_index("row") * lax.axis_size("col") + lax.axis_index("col")) * ROWS
    last = PAIRS - 1
    done = ROWS - 2
    copies = [pltpu.make_async_copy(out.at[pl.ds(2 * p, 2)], final.at[pl.ds(2 * p, 2)], sem.at[p]) for p in range(last)]
    copies.append(pltpu.make_async_copy(out.at[done, pl.ds(0, 2)], final.at[done, pl.ds(0, 2)], sem.at[last]))
    copies.append(pltpu.make_async_copy(out.at[done + 1, pl.ds(0, 1)], final.at[done + 1, pl.ds(0, 1)], sem.at[last + 1]))
    for copy in copies:
        copy.start()
    for d in range(1, H + 1):
        at = WINDOW - 2 * d - 2
        total = window_product(left, right_hi, right_lo, last, d, at, at + 2)
        for r, s, m in places(d):
            piece = quarter(total, r, s) * keep_weight(keep_s, done + r, m, first_row, n_part * ROWS)
            tail[r, m] = piece if d == H else out[done + r, m] + piece
    n = 2 * H + 1
    more = [
        pltpu.make_async_copy(tail.at[0, pl.ds(2, n - 2)], final.at[done, pl.ds(2, n - 2)], sem.at[last + 2]),
        pltpu.make_async_copy(tail.at[1, pl.ds(1, n - 1)], final.at[done + 1, pl.ds(1, n - 1)], sem.at[last + 3]),
    ]
    for copy in more:
        copy.start()
    for copy in copies + more:
        copy.wait()


def kernel(
    up, mask_s, mask_v, keep_s, out, right_hi, right_lo, left,
    own, behind, ahead, mask_b, mask_a,
    load_sem, send_sem, recv_sem, pass_send, pass_recv, mask_send, mask_recv, ready,
):
    row, col, layer = lax.axis_index("row"), lax.axis_index("col"), lax.axis_index("layer")
    n_col = lax.axis_size("col")
    n_part = lax.axis_size("row") * n_col
    total_rows = n_part * ROWS
    part = row * n_col + col
    after = lax.rem(part + 1, n_part)
    before = lax.rem(part + n_part - 1, n_part)
    nxt = (after // n_col, lax.rem(after, n_col), layer)
    prv = (before // n_col, lax.rem(before, n_col), layer)
    sib = (row, col, 1 - layer)
    first_row = part * ROWS
    half = pl.ds(pl.multiple_of(layer * HALF, HALF), HALF)

    def head(j):
        return pltpu.make_async_remote_copy(
            src_ref=up.at[j, :, half, :], dst_ref=ahead.at[j, :, half, :],
            send_sem=send_sem.at[j], recv_sem=recv_sem.at[j], device_id=prv, device_id_type=MESH)

    def tail(a):
        return pltpu.make_async_remote_copy(
            src_ref=up.at[ROWS - 1 - a, pl.ds(a + 1, H - a), half, :],
            dst_ref=behind.at[a, pl.ds(0, H - a), half, :],
            send_sem=send_sem.at[H + a], recv_sem=recv_sem.at[H + a], device_id=nxt, device_id_type=MESH)

    def head_pass(j):
        return pltpu.make_async_remote_copy(
            src_ref=ahead.at[j, :, half, :], dst_ref=ahead.at[j, :, half, :],
            send_sem=pass_send.at[j], recv_sem=pass_recv.at[j], device_id=sib, device_id_type=MESH)

    def tail_pass(a):
        return pltpu.make_async_remote_copy(
            src_ref=behind.at[a, pl.ds(0, H - a), half, :], dst_ref=behind.at[a, pl.ds(0, H - a), half, :],
            send_sem=pass_send.at[H + a], recv_sem=pass_recv.at[H + a], device_id=sib, device_id_type=MESH)

    mask_head = pltpu.make_async_remote_copy(
        src_ref=mask_v, dst_ref=mask_a, send_sem=mask_send.at[0], recv_sem=mask_recv.at[0],
        device_id=prv, device_id_type=MESH)
    mask_tail = pltpu.make_async_remote_copy(
        src_ref=mask_v, dst_ref=mask_b, send_sem=mask_send.at[1], recv_sem=mask_recv.at[1],
        device_id=nxt, device_id_type=MESH)
    load = pltpu.make_async_copy(up, own, load_sem)

    barrier = pltpu.get_barrier_semaphore()
    pl.semaphore_signal(barrier, inc=1, device_id=nxt, device_id_type=MESH)
    pl.semaphore_signal(barrier, inc=1, device_id=sib, device_id_type=MESH)
    load.start()
    pl.semaphore_wait(barrier, 2)
    mask_head.start()
    for j in range(H):
        head(j).start()
    pl.semaphore_signal(ready, inc=1, device_id=prv, device_id_type=MESH)

    zero_right = jnp.zeros((B, B), jnp.bfloat16)
    zero_left = jnp.zeros((HALF, B), jnp.bfloat16)

    def clear(pair, carry):
        for ref in (right_hi, right_lo):
            ref[pair, pl.ds(0, B), pl.ds(B, B)] = zero_right
            ref[pair, pl.ds((WINDOW - 1) * B, B), pl.ds(0, B)] = zero_right
        return carry

    lax.fori_loop(0, 2 * PAIRS, clear, 0)

    def clear_left(pair, carry):
        for base in (0, B):
            left[pair, pl.ds(base, HALF), pl.ds((WINDOW - 1) * B, B)] = zero_left
            left[pair, pl.ds(base + HALF, HALF), pl.ds(0, B)] = zero_left
        return carry

    lax.fori_loop(0, PAIRS, clear_left, 0)

    load.wait()

    def place_right(pair, r, k, x):
        hi, lo = split(x)
        at = pair + (r + k) // 2
        rows = pl.ds((r + H - 2 * ((r + k) // 2)) * B, B)
        lanes = pl.ds(((r + k) % 2) * B, B)
        right_hi[at, rows, lanes] = hi
        right_lo[at, rows, lanes] = lo

    def place_right_t(pair, r, k, xt):
        hi, lo = split(xt)
        rows = pl.ds((r + k + H) * B, B)
        right_hi[pair, rows, pl.ds(r * B, B)] = hi
        right_lo[pair, rows, pl.ds(r * B, B)] = lo

    def my_half(x):
        return jnp.where(layer == 0, x[:HALF], x[HALF:])

    def place_left(pair, r, offset, xh):
        hi, lo = split(xh)
        lanes = pl.ds((r + offset + H) * B, B)
        left[pair, pl.ds(r * HALF, HALF), lanes] = hi
        left[pair, pl.ds(B + r * HALF, HALF), lanes] = lo

    def own_pair(pair, carry):
        for r in range(2):
            for k in range(H + 1):
                j = 2 * pair + r
                inside = first_row + j + k < total_rows
                if k > 0:
                    inside = inside & (mask_s[k, j] == 1)
                weight = jnp.where(inside, jnp.float32(1.0), jnp.float32(0.0))
                x = masked(weight, own[j, k])
                xt = x.T
                if k == 0:
                    x = 0.5 * (x + xt)
                place_right(pair, r, k, x)
                place_left(pair, r, k, my_half(x))
                if k > 0:
                    place_right_t(pair, r, k, xt)
                    own_row = pair + (r + k) // 2

                    @pl.when(own_row < PAIRS)
                    def _():
                        place_left(own_row, (r + k) % 2, -k, my_half(xt))

        return carry

    lax.fori_loop(0, PAIRS, own_pair, 0)
    pl.semaphore_wait(ready, 1)
    mask_tail.start()
    for a in range(H):
        tail(a).start()

    def multiply(pair, d, lo_block, hi_block):
        return window_product(left, right_hi, right_lo, pair, d, lo_block, hi_block)

    def emit(pair, d, total, add):
        for r, s, m in places(d):
            i = 2 * pair + r
            piece = quarter(total, r, s) * keep_weight(keep_s, i, m, first_row, total_rows)
            if add:
                out[i, m] += piece
            else:
                out[i, m] = piece

    def own_low(d, first):
        def body(pair, carry):
            emit(pair, d, multiply(pair, d, 0, WINDOW - 2 * d), False)
            return carry

        lax.fori_loop(first, H // 2, body, 0)

    for d in range(H + 1):
        own_low(d, max(0, H // 2 - d))
    for pair in range(H // 2, PAIRS):
        for d in range(H + 1):
            c = pair + d
            if c < PAIRS:
                emit(pair, d, multiply(pair, d, 0, WINDOW - 2 * d), False)
            elif c < PAIRS + H // 2:
                emit(pair, d, multiply(pair, d, 0, 2 * (PAIRS + H // 2 - c)), False)

    for a in range(H):
        tail(a).wait_recv()
        tail_pass(a).start()
    mask_tail.wait_recv()
    for a in range(H):
        tail_pass(a).wait_recv()
        j = -1 - a
        pair, r = j // 2, j % 2
        for k in range(a + 1, H + 1):
            present = (mask_b[pl.ds(k, 1), pl.ds(ROWS + j, 1)] == 1) & (part > 0)
            x = masked(jnp.where(present, jnp.float32(1.0), jnp.float32(0.0)), behind[a, k - a - 1])
            place_right(pair, r, k, x)
            place_left(pair + (r + k) // 2, (r + k) % 2, -k, my_half(x.T))
    for pair in range(H // 2):
        for d in range(H // 2 - pair):
            emit(pair, d, multiply(pair, d, 0, WINDOW - 2 * d), False)

    mask_head.wait_recv()
    for q in range(H // 2):
        for r in range(2):
            j = 2 * q + r
            head(j).wait_recv()
            head_pass(j).start()
            head_pass(j).wait_recv()
            for k in range(H + 1):
                present = first_row + ROWS + j + k < total_rows
                weight = jnp.where(present, jnp.float32(1.0), jnp.float32(0.0))
                if k > 0:
                    weight = jnp.where(mask_a[pl.ds(k, 1), pl.ds(j, 1)] == 1, weight, jnp.float32(0.0))
                x = masked(weight, ahead[j, k])
                if k == 0:
                    x = 0.5 * (x + x.T)
                place_right(PAIRS + q, r, k, x)
                if 0 < k < H - j:
                    place_right_t(PAIRS + q, r, k, x.T)
        if q == H // 2 - 1:
            break
        for pair in range(H // 2 + q, PAIRS):
            for c in range(PAIRS, PAIRS + q + H // 2 + 1):
                d = c - pair
                at = 2 * (PAIRS + q - (c - H // 2))
                first = c >= PAIRS + H // 2 and q == c - PAIRS - H // 2
                emit(pair, d, multiply(pair, d, at, at + 2), not first)

    for j in range(H):
        head(j).wait_send()
        tail(j).wait_send()
        head_pass(j).wait_send()
        tail_pass(j).wait_send()
    mask_head.wait_send()
    mask_tail.wait_send()


def on_device(upper, block_mask, keep_mask):
    f32, bf16 = jnp.float32, jnp.bfloat16
    window = WINDOW * B
    spread = pl.pallas_call(
        kernel,
        out_shape=(
            pltpu.VMEM((ROWS, 2 * H + 1, HALF, B), f32),
            pltpu.VMEM((2 * PAIRS, window, 2 * B), bf16),
            pltpu.VMEM((2 * PAIRS, window, 2 * B), bf16),
            pltpu.VMEM((PAIRS, 2 * B, window), bf16),
        ),
        in_specs=[
            pl.BlockSpec(memory_space=pltpu.HBM),
            pl.BlockSpec(memory_space=pltpu.SMEM),
            pl.BlockSpec(memory_space=pltpu.VMEM),
            pl.BlockSpec(memory_space=pltpu.SMEM),
        ],
        out_specs=[pl.BlockSpec(memory_space=pltpu.VMEM)] * 4,
        scratch_shapes=[
            pltpu.VMEM((ROWS, H + 1, B, B), f32),
            pltpu.VMEM((H, H, B, B), f32),
            pltpu.VMEM((H, H + 1, B, B), f32),
            pltpu.VMEM((H + 1, ROWS), jnp.int32),
            pltpu.VMEM((H + 1, ROWS), jnp.int32),
            pltpu.SemaphoreType.DMA,
            pltpu.SemaphoreType.DMA((2 * H,)),
            pltpu.SemaphoreType.DMA((2 * H,)),
            pltpu.SemaphoreType.DMA((2 * H,)),
            pltpu.SemaphoreType.DMA((2 * H,)),
            pltpu.SemaphoreType.DMA((2,)),
            pltpu.SemaphoreType.DMA((2,)),
            pltpu.SemaphoreType.REGULAR,
        ],
        compiler_params=pltpu.CompilerParams(
            collective_id=0, has_side_effects=True, vmem_limit_bytes=18 * 2**20
        ),
    )
    masks = block_mask.T
    parts = spread(upper, masks, masks, keep_mask)
    parts = [pltpu.with_memory_space_constraint(x, pltpu.VMEM) for x in parts]
    return pl.pallas_call(
        finish,
        out_shape=jax.ShapeDtypeStruct((ROWS, 2 * H + 1, HALF, B), f32),
        in_specs=[pl.BlockSpec(memory_space=pltpu.VMEM)] * 4 + [pl.BlockSpec(memory_space=pltpu.SMEM)],
        out_specs=pl.BlockSpec(memory_space=pltpu.HBM),
        scratch_shapes=[
            pltpu.VMEM((2, 2 * H + 1, HALF, B), f32),
            pltpu.SemaphoreType.DMA((PAIRS + 3,)),
        ],
        compiler_params=pltpu.CompilerParams(vmem_limit_bytes=8 * 2**20),
    )(*parts, keep_mask)


def solution(mesh):
    in_specs = (
        P(("row", "col"), None, None, None),
        P(("row", "col"), None),
        P(("row", "col"), None),
    )
    out_specs = P(("row", "col"), None, "layer", None)
    return jax.shard_map(
        on_device, mesh=mesh, in_specs=in_specs, out_specs=out_specs, check_vma=False
    )
```

```python
import functools

import jax
import jax.numpy as jnp
from jax import lax
from jax.experimental import pallas as pl
from jax.experimental.pallas import tpu as pltpu
from jax.sharding import PartitionSpec as P

MESH = pl.DeviceIdType.MESH
B = 128
H = 6
ROWS = 12
PAIRS = ROWS // 2
WINDOW = 2 * H + 2
HALF = B // 2


def masked(weight, block):
    return block * weight


def split(x):
    hi = x.astype(jnp.bfloat16)
    lo = (x - hi.astype(jnp.float32)).astype(jnp.bfloat16)
    return hi, lo


def window_product(left, right_hi, right_lo, pair, d, lo_block, hi_block):
    n = (hi_block - lo_block) * B
    lanes = pl.ds((2 * d + lo_block) * B, n)
    rows = pl.ds(lo_block * B, n)
    both = jnp.dot(left[pair, :, lanes], right_hi[pair + d, rows, :], preferred_element_type=jnp.float32)
    rest = jnp.dot(left[pair, pl.ds(0, B), lanes], right_lo[pair + d, rows, :], preferred_element_type=jnp.float32)
    return both[:B] + (both[B:] + rest)


def places(d):
    spots = [(r, s, 2 * d + s - r) for r in range(2) for s in range(2)]
    return [spot for spot in spots if 0 <= spot[2] <= 2 * H]


def quarter(total, r, s):
    return total[r * HALF : (r + 1) * HALF, s * B : (s + 1) * B]


def keep_weight(keep_s, i, m, first_row, total_rows):
    kept = (keep_s[i, m] == 1) & (first_row + i + m < total_rows)
    return jnp.where(kept, jnp.float32(1.0), jnp.float32(0.0))


def finish(out, right_hi, right_lo, left, keep_s, final, tail, sem):
    n_part = lax.axis_size("row") * lax.axis_size("col")
    first_row = (lax.axis_index("row") * lax.axis_size("col") + lax.axis_index("col")) * ROWS
    last = PAIRS - 1
    done = ROWS - 2
    copies = [pltpu.make_async_copy(out.at[pl.ds(2 * p, 2)], final.at[pl.ds(2 * p, 2)], sem.at[p]) for p in range(last)]
    copies.append(pltpu.make_async_copy(out.at[done, pl.ds(0, 2)], final.at[done, pl.ds(0, 2)], sem.at[last]))
    copies.append(pltpu.make_async_copy(out.at[done + 1, pl.ds(0, 1)], final.at[done + 1, pl.ds(0, 1)], sem.at[last + 1]))
    for copy in copies:
        copy.start()
    for d in range(1, H + 1):
        at = WINDOW - 2 * d - 2
        total = window_product(left, right_hi, right_lo, last, d, at, at + 2)
        for r, s, m in places(d):
            piece = quarter(total, r, s) * keep_weight(keep_s, done + r, m, first_row, n_part * ROWS)
            tail[r, m] = piece if d == H else out[done + r, m] + piece
    n = 2 * H + 1
    more = [
        pltpu.make_async_copy(tail.at[0, pl.ds(2, n - 2)], final.at[done, pl.ds(2, n - 2)], sem.at[last + 2]),
        pltpu.make_async_copy(tail.at[1, pl.ds(1, n - 1)], final.at[done + 1, pl.ds(1, n - 1)], sem.at[last + 3]),
    ]
    for copy in more:
        copy.start()
    for copy in copies + more:
        copy.wait()


def kernel(
    up, mask, keep, out, right_hi, right_lo, left,
    own, behind, ahead, mask_b, mask_a, mask_s, keep_s, raw, folded, corner, folded_a, corner_a,
    load_sem, send_sem, recv_sem, pass_send, pass_recv, mask_send, mask_recv, ready,
):
    row, col, layer = lax.axis_index("row"), lax.axis_index("col"), lax.axis_index("layer")
    n_col = lax.axis_size("col")
    n_part = lax.axis_size("row") * n_col
    total_rows = n_part * ROWS
    part = row * n_col + col
    after = lax.rem(part + 1, n_part)
    before = lax.rem(part + n_part - 1, n_part)
    nxt = (after // n_col, lax.rem(after, n_col), layer)
    prv = (before // n_col, lax.rem(before, n_col), layer)
    sib = (row, col, 1 - layer)
    first_row = part * ROWS
    half = pl.ds(pl.multiple_of(layer * HALF, HALF), HALF)

    def head(j):
        return pltpu.make_async_remote_copy(
            src_ref=up.at[j, pl.ds(1, H), half, :], dst_ref=ahead.at[j, :, half, :],
            send_sem=send_sem.at[j], recv_sem=recv_sem.at[j], device_id=prv, device_id_type=MESH)

    def tail(a):
        return pltpu.make_async_remote_copy(
            src_ref=up.at[ROWS - 1 - a, pl.ds(a + 1, H - a), half, :],
            dst_ref=behind.at[a, pl.ds(0, H - a), half, :],
            send_sem=send_sem.at[H + a], recv_sem=recv_sem.at[H + a], device_id=nxt, device_id_type=MESH)

    def head_pass(j):
        return pltpu.make_async_remote_copy(
            src_ref=ahead.at[j, :, half, :], dst_ref=ahead.at[j, :, half, :],
            send_sem=pass_send.at[j], recv_sem=pass_recv.at[j], device_id=sib, device_id_type=MESH)

    def tail_pass(a):
        return pltpu.make_async_remote_copy(
            src_ref=behind.at[a, pl.ds(0, H - a), half, :], dst_ref=behind.at[a, pl.ds(0, H - a), half, :],
            send_sem=pass_send.at[H + a], recv_sem=pass_recv.at[H + a], device_id=sib, device_id_type=MESH)

    mask_head = pltpu.make_async_remote_copy(
        src_ref=mask, dst_ref=mask_a, send_sem=mask_send.at[0], recv_sem=mask_recv.at[0],
        device_id=prv, device_id_type=MESH)
    mask_tail = pltpu.make_async_remote_copy(
        src_ref=mask, dst_ref=mask_b, send_sem=mask_send.at[1], recv_sem=mask_recv.at[1],
        device_id=nxt, device_id_type=MESH)
    fold_half = pl.ds(pl.multiple_of(layer * (HALF // 2), HALF // 2), HALF // 2)
    fold_send = pltpu.make_async_remote_copy(
        src_ref=folded.at[:, fold_half, :], dst_ref=folded_a.at[:, fold_half, :],
        send_sem=mask_send.at[2], recv_sem=mask_recv.at[2], device_id=prv, device_id_type=MESH)
    fold_pass = pltpu.make_async_remote_copy(
        src_ref=folded_a.at[:, fold_half, :], dst_ref=folded_a.at[:, fold_half, :],
        send_sem=mask_send.at[3], recv_sem=mask_recv.at[3], device_id=sib, device_id_type=MESH)
    corner_send = pltpu.make_async_remote_copy(
        src_ref=corner, dst_ref=corner_a, send_sem=mask_send.at[4], recv_sem=mask_recv.at[4],
        device_id=prv, device_id_type=MESH)
    load_diagonal = pltpu.make_async_copy(up.at[pl.ds(0, H), 0], raw, load_sem.at[0])
    load = pltpu.make_async_copy(up, own, load_sem.at[1])
    load_mask = pltpu.make_async_copy(mask, mask_s, load_sem.at[2])
    load_keep = pltpu.make_async_copy(keep, keep_s, load_sem.at[3])

    barrier = pltpu.get_barrier_semaphore()
    pl.semaphore_signal(barrier, inc=1, device_id=nxt, device_id_type=MESH)
    pl.semaphore_signal(barrier, inc=1, device_id=sib, device_id_type=MESH)
    load_diagonal.start()
    load_mask.start()
    load_keep.start()
    load.start()
    pl.semaphore_wait(barrier, 2)
    mask_head.start()
    for j in range(H - 2):
        head(j).start()
    pl.semaphore_signal(ready, inc=1, device_id=prv, device_id_type=MESH)

    load_diagonal.wait()
    row_at = lax.broadcasted_iota(jnp.int32, (HALF, B), 0)
    lane_at = lax.broadcasted_iota(jnp.int32, (HALF, B), 1)
    corner[...] = jnp.zeros_like(corner)
    for j in range(H):
        x = raw[j]
        x = 0.5 * (x + x.T)
        low = x[HALF:]
        folded[j] = jnp.where(lane_at < row_at, pltpu.roll(low, HALF, 1), x[:HALF])
        corner[pl.ds(j, 1), :] = jnp.sum(jnp.where(lane_at == row_at + HALF, low, 0.0), axis=0, keepdims=True)
    fold_send.start()
    corner_send.start()
    for j in range(H - 2, H):
        head(j).start()

    zero_right = jnp.zeros((B, B), jnp.bfloat16)
    zero_left = jnp.zeros((HALF, B), jnp.bfloat16)

    def clear(pair, carry):
        for ref in (right_hi, right_lo):
            ref[pair, pl.ds(0, B), pl.ds(B, B)] = zero_right
            ref[pair, pl.ds((WINDOW - 1) * B, B), pl.ds(0, B)] = zero_right
        return carry

    lax.fori_loop(0, 2 * PAIRS, clear, 0)

    def clear_left(pair, carry):
        for base in (0, B):
            left[pair, pl.ds(base, HALF), pl.ds((WINDOW - 1) * B, B)] = zero_left
            left[pair, pl.ds(base + HALF, HALF), pl.ds(0, B)] = zero_left
        return carry

    lax.fori_loop(0, PAIRS, clear_left, 0)

    pl.semaphore_wait(ready, 1)
    mask_tail.start()
    for a in range(H):
        tail(a).start()
    load_mask.wait()
    load_keep.wait()
    load.wait()

    def place_right(pair, r, k, x):
        hi, lo = split(x)
        at = pair + (r + k) // 2
        rows = pl.ds((r + H - 2 * ((r + k) // 2)) * B, B)
        lanes = pl.ds(((r + k) % 2) * B, B)
        right_hi[at, rows, lanes] = hi
        right_lo[at, rows, lanes] = lo

    def place_right_t(pair, r, k, xt):
        hi, lo = split(xt)
        rows = pl.ds((r + k + H) * B, B)
        right_hi[pair, rows, pl.ds(r * B, B)] = hi
        right_lo[pair, rows, pl.ds(r * B, B)] = lo

    def my_half(x):
        return jnp.where(layer == 0, x[:HALF], x[HALF:])

    def place_left(pair, r, offset, xh):
        hi, lo = split(xh)
        lanes = pl.ds((r + offset + H) * B, B)
        left[pair, pl.ds(r * HALF, HALF), lanes] = hi
        left[pair, pl.ds(B + r * HALF, HALF), lanes] = lo

    def own_pair(pair, carry):
        for r in range(2):
            for k in range(H + 1):
                j = 2 * pair + r
                inside = first_row + j + k < total_rows
                if k > 0:
                    inside = inside & (mask_s[k, j] == 1)
                weight = jnp.where(inside, jnp.float32(1.0), jnp.float32(0.0))
                x = masked(weight, own[j, k])
                xt = x.T
                if k == 0:
                    x = 0.5 * (x + xt)
                place_right(pair, r, k, x)
                place_left(pair, r, k, my_half(x))
                if k > 0:
                    place_right_t(pair, r, k, xt)
                    own_row = pair + (r + k) // 2

                    @pl.when(own_row < PAIRS)
                    def _():
                        place_left(own_row, (r + k) % 2, -k, my_half(xt))

        return carry

    lax.fori_loop(0, PAIRS, own_pair, 0)

    def multiply(pair, d, lo_block, hi_block):
        return window_product(left, right_hi, right_lo, pair, d, lo_block, hi_block)

    def emit(pair, d, total, add):
        for r, s, m in places(d):
            i = 2 * pair + r
            piece = quarter(total, r, s) * keep_weight(keep_s, i, m, first_row, total_rows)
            if add:
                out[i, m] += piece
            else:
                out[i, m] = piece

    def own_low(d, first):
        def body(pair, carry):
            emit(pair, d, multiply(pair, d, 0, WINDOW - 2 * d), False)
            return carry

        lax.fori_loop(first, H // 2, body, 0)

    for d in range(H + 1):
        own_low(d, max(0, H // 2 - d))
    for pair in range(H // 2, PAIRS):
        for d in range(H + 1):
            c = pair + d
            if c < PAIRS:
                emit(pair, d, multiply(pair, d, 0, WINDOW - 2 * d), False)
            elif c < PAIRS + H // 2:
                emit(pair, d, multiply(pair, d, 0, 2 * (PAIRS + H // 2 - c)), False)

    for a in range(H):
        tail(a).wait_recv()
        tail_pass(a).start()
    for j in range(2):
        head(j).wait_recv()
        head_pass(j).start()
    mask_tail.wait_recv()
    for a in range(H):
        tail_pass(a).wait_recv()
        j = -1 - a
        pair, r = j // 2, j % 2
        for k in range(a + 1, H + 1):
            present = (mask_b[pl.ds(k, 1), pl.ds(ROWS + j, 1)] == 1) & (part > 0)
            x = masked(jnp.where(present, jnp.float32(1.0), jnp.float32(0.0)), behind[a, k - a - 1])
            place_right(pair, r, k, x)
            place_left(pair + (r + k) // 2, (r + k) % 2, -k, my_half(x.T))
    for pair in range(H // 2):
        for d in range(H // 2 - pair):
            emit(pair, d, multiply(pair, d, 0, WINDOW - 2 * d), False)

    mask_head.wait_recv()
    corner_send.wait_recv()
    row_at = lax.broadcasted_iota(jnp.int32, (B, B), 0)
    lane_at = lax.broadcasted_iota(jnp.int32, (B, B), 1)
    top, leading = row_at < HALF, lane_at < HALF
    as_sent = (top & (~leading | (row_at <= lane_at))) | (~top & ~leading & (row_at > lane_at))
    on_corner = ~top & (row_at == lane_at)

    def unfold(j):
        x = folded_a[j]
        x = jnp.concatenate([x, pltpu.roll(x, HALF, 1)], axis=0)
        return jnp.where(on_corner, corner_a[pl.ds(j, 1), :], jnp.where(as_sent, x, x.T))

    def take(j):
        head(j).wait_recv()
        head_pass(j).start()

    def place_row(j):
        q, r = j // 2, j % 2
        head_pass(j).wait_recv()
        for k in range(H + 1):
            present = first_row + ROWS + j + k < total_rows
            weight = jnp.where(present, jnp.float32(1.0), jnp.float32(0.0))
            if k > 0:
                weight = jnp.where(mask_a[pl.ds(k, 1), pl.ds(j, 1)] == 1, weight, jnp.float32(0.0))
            x = masked(weight, ahead[j, k - 1] if k > 0 else unfold(j))
            place_right(PAIRS + q, r, k, x)
            if 0 < k < H - j:
                place_right_t(PAIRS + q, r, k, x.T)

    def add_terms(q):
        for pair in range(H // 2 + q, PAIRS):
            for c in range(PAIRS, PAIRS + q + H // 2 + 1):
                d = c - pair
                at = 2 * (PAIRS + q - (c - H // 2))
                first = c >= PAIRS + H // 2 and q == c - PAIRS - H // 2
                emit(pair, d, multiply(pair, d, at, at + 2), not first)

    take(2)
    fold_send.wait_recv()
    fold_pass.start()
    fold_pass.wait_recv()
    place_row(0)
    place_row(1)
    take(3)
    add_terms(0)
    place_row(2)
    take(4)
    place_row(3)
    add_terms(1)
    take(5)
    place_row(4)
    place_row(5)

    for j in range(H):
        head(j).wait_send()
        tail(j).wait_send()
        head_pass(j).wait_send()
        tail_pass(j).wait_send()
    for copy in (mask_head, mask_tail, fold_send, fold_pass, corner_send):
        copy.wait_send()


def on_device(upper, block_mask, keep_mask):
    f32, bf16 = jnp.float32, jnp.bfloat16
    window = WINDOW * B
    spread = pl.pallas_call(
        kernel,
        out_shape=(
            pltpu.VMEM((ROWS, 2 * H + 1, HALF, B), f32),
            pltpu.VMEM((2 * PAIRS, window, 2 * B), bf16),
            pltpu.VMEM((2 * PAIRS, window, 2 * B), bf16),
            pltpu.VMEM((PAIRS, 2 * B, window), bf16),
        ),
        in_specs=[
            pl.BlockSpec(memory_space=pltpu.HBM),
            pl.BlockSpec(memory_space=pltpu.HBM),
            pl.BlockSpec(memory_space=pltpu.HBM),
        ],
        out_specs=[pl.BlockSpec(memory_space=pltpu.VMEM)] * 4,
        scratch_shapes=[
            pltpu.VMEM((ROWS, H + 1, B, B), f32),
            pltpu.VMEM((H, H, B, B), f32),
            pltpu.VMEM((H, H, B, B), f32),
            pltpu.VMEM((H + 1, ROWS), jnp.int32),
            pltpu.VMEM((H + 1, ROWS), jnp.int32),
            pltpu.SMEM((H + 1, ROWS), jnp.int32),
            pltpu.SMEM((ROWS, 2 * H + 1), jnp.int32),
            pltpu.VMEM((H, B, B), f32),
            pltpu.VMEM((H, HALF, B), f32),
            pltpu.VMEM((8, B), f32),
            pltpu.VMEM((H, HALF, B), f32),
            pltpu.VMEM((8, B), f32),
            pltpu.SemaphoreType.DMA((4,)),
            pltpu.SemaphoreType.DMA((2 * H,)),
            pltpu.SemaphoreType.DMA((2 * H,)),
            pltpu.SemaphoreType.DMA((2 * H,)),
            pltpu.SemaphoreType.DMA((2 * H,)),
            pltpu.SemaphoreType.DMA((5,)),
            pltpu.SemaphoreType.DMA((5,)),
            pltpu.SemaphoreType.REGULAR,
        ],
        compiler_params=pltpu.CompilerParams(
            collective_id=0, has_side_effects=True, vmem_limit_bytes=18 * 2**20
        ),
    )
    held = [pltpu.with_memory_space_constraint(x, pltpu.HBM) for x in (upper, block_mask.T, keep_mask)]
    parts = spread(*held)
    parts = [pltpu.with_memory_space_constraint(x, pltpu.VMEM) for x in parts]
    return pl.pallas_call(
        finish,
        out_shape=jax.ShapeDtypeStruct((ROWS, 2 * H + 1, HALF, B), f32),
        in_specs=[pl.BlockSpec(memory_space=pltpu.VMEM)] * 4 + [pl.BlockSpec(memory_space=pltpu.SMEM)],
        out_specs=pl.BlockSpec(memory_space=pltpu.HBM),
        scratch_shapes=[
            pltpu.VMEM((2, 2 * H + 1, HALF, B), f32),
            pltpu.SemaphoreType.DMA((PAIRS + 3,)),
        ],
        compiler_params=pltpu.CompilerParams(vmem_limit_bytes=8 * 2**20),
    )(*parts, keep_mask)


def solution(mesh):
    in_specs = (
        P(("row", "col"), None, None, None),
        P(("row", "col"), None),
        P(("row", "col"), None),
    )
    out_specs = P(("row", "col"), None, "layer", None)
    return jax.shard_map(
        on_device, mesh=mesh, in_specs=in_specs, out_specs=out_specs, check_vma=False
    )
```

```python
import functools

import jax
import jax.numpy as jnp
from jax import lax
from jax.experimental import pallas as pl
from jax.experimental.pallas import tpu as pltpu
from jax.sharding import PartitionSpec as P

MESH = pl.DeviceIdType.MESH
B = 128
H = 6
ROWS = 12
PAIRS = ROWS // 2
WINDOW = 2 * H + 2
HALF = B // 2


def masked(weight, block):
    return block * weight


def split(x):
    hi = x.astype(jnp.bfloat16)
    lo = (x - hi.astype(jnp.float32)).astype(jnp.bfloat16)
    return hi, lo


def window_product(left, right_hi, right_lo, pair, d, lo_block, hi_block):
    n = (hi_block - lo_block) * B
    lanes = pl.ds((2 * d + lo_block) * B, n)
    rows = pl.ds(lo_block * B, n)
    both = jnp.dot(left[pair, :, lanes], right_hi[pair + d, rows, :], preferred_element_type=jnp.float32)
    rest = jnp.dot(left[pair, pl.ds(0, B), lanes], right_lo[pair + d, rows, :], preferred_element_type=jnp.float32)
    return both[:B] + (both[B:] + rest)


def places(d):
    spots = [(r, s, 2 * d + s - r) for r in range(2) for s in range(2)]
    return [spot for spot in spots if 0 <= spot[2] <= 2 * H]


def quarter(total, r, s):
    return total[r * HALF : (r + 1) * HALF, s * B : (s + 1) * B]


def keep_weight(keep_s, i, m, first_row, total_rows):
    kept = (keep_s[i, m] == 1) & (first_row + i + m < total_rows)
    return jnp.where(kept, jnp.float32(1.0), jnp.float32(0.0))


def finish(out, right_hi, right_lo, left, keep, final, tail, keep_s, sem):
    n_part = lax.axis_size("row") * lax.axis_size("col")
    first_row = (lax.axis_index("row") * lax.axis_size("col") + lax.axis_index("col")) * ROWS
    last = PAIRS - 1
    done = ROWS - 2
    copies = [pltpu.make_async_copy(out.at[pl.ds(2 * p, 2)], final.at[pl.ds(2 * p, 2)], sem.at[p]) for p in range(last)]
    copies.append(pltpu.make_async_copy(out.at[done, pl.ds(0, 2)], final.at[done, pl.ds(0, 2)], sem.at[last]))
    copies.append(pltpu.make_async_copy(out.at[done + 1, pl.ds(0, 1)], final.at[done + 1, pl.ds(0, 1)], sem.at[last + 1]))
    load_keep = pltpu.make_async_copy(keep, keep_s, sem.at[last + 4])
    load_keep.start()
    for copy in copies:
        copy.start()
    load_keep.wait()
    for d in range(1, H + 1):
        at = WINDOW - 2 * d - 2
        total = window_product(left, right_hi, right_lo, last, d, at, at + 2)
        for r, s, m in places(d):
            piece = quarter(total, r, s) * keep_weight(keep_s, done + r, m, first_row, n_part * ROWS)
            tail[r, m] = piece if d == H else out[done + r, m] + piece
    n = 2 * H + 1
    more = [
        pltpu.make_async_copy(tail.at[0, pl.ds(2, n - 2)], final.at[done, pl.ds(2, n - 2)], sem.at[last + 2]),
        pltpu.make_async_copy(tail.at[1, pl.ds(1, n - 1)], final.at[done + 1, pl.ds(1, n - 1)], sem.at[last + 3]),
    ]
    for copy in more:
        copy.start()
    for copy in copies + more:
        copy.wait()


def kernel(
    up, mask, keep, out, right_hi, right_lo, left,
    own, behind, ahead, mask_b, mask_a, mask_s, keep_s, raw, folded, corner, folded_a, corner_a,
    load_sem, send_sem, recv_sem, pass_send, pass_recv, mask_send, mask_recv, ready,
):
    row, col, layer = lax.axis_index("row"), lax.axis_index("col"), lax.axis_index("layer")
    n_col = lax.axis_size("col")
    n_part = lax.axis_size("row") * n_col
    total_rows = n_part * ROWS
    part = row * n_col + col
    after = lax.rem(part + 1, n_part)
    before = lax.rem(part + n_part - 1, n_part)
    nxt = (after // n_col, lax.rem(after, n_col), layer)
    prv = (before // n_col, lax.rem(before, n_col), layer)
    sib = (row, col, 1 - layer)
    first_row = part * ROWS
    half = pl.ds(pl.multiple_of(layer * HALF, HALF), HALF)

    def head(j):
        return pltpu.make_async_remote_copy(
            src_ref=up.at[j, pl.ds(1, H), half, :], dst_ref=ahead.at[j, :, half, :],
            send_sem=send_sem.at[j], recv_sem=recv_sem.at[j], device_id=prv, device_id_type=MESH)

    def tail(a):
        return pltpu.make_async_remote_copy(
            src_ref=up.at[ROWS - 1 - a, pl.ds(a + 1, H - a), half, :],
            dst_ref=behind.at[a, pl.ds(0, H - a), half, :],
            send_sem=send_sem.at[H + a], recv_sem=recv_sem.at[H + a], device_id=nxt, device_id_type=MESH)

    def head_pass(j):
        return pltpu.make_async_remote_copy(
            src_ref=ahead.at[j, :, half, :], dst_ref=ahead.at[j, :, half, :],
            send_sem=pass_send.at[j], recv_sem=pass_recv.at[j], device_id=sib, device_id_type=MESH)

    def tail_pass(a):
        return pltpu.make_async_remote_copy(
            src_ref=behind.at[a, pl.ds(0, H - a), half, :], dst_ref=behind.at[a, pl.ds(0, H - a), half, :],
            send_sem=pass_send.at[H + a], recv_sem=pass_recv.at[H + a], device_id=sib, device_id_type=MESH)

    mask_head = pltpu.make_async_remote_copy(
        src_ref=mask, dst_ref=mask_a, send_sem=mask_send.at[0], recv_sem=mask_recv.at[0],
        device_id=prv, device_id_type=MESH)
    mask_tail = pltpu.make_async_remote_copy(
        src_ref=mask, dst_ref=mask_b, send_sem=mask_send.at[1], recv_sem=mask_recv.at[1],
        device_id=nxt, device_id_type=MESH)
    fold_half = pl.ds(pl.multiple_of(layer * (HALF // 2), HALF // 2), HALF // 2)
    fold_send = pltpu.make_async_remote_copy(
        src_ref=folded.at[:, fold_half, :], dst_ref=folded_a.at[:, fold_half, :],
        send_sem=mask_send.at[2], recv_sem=mask_recv.at[2], device_id=prv, device_id_type=MESH)
    fold_pass = pltpu.make_async_remote_copy(
        src_ref=folded_a.at[:, fold_half, :], dst_ref=folded_a.at[:, fold_half, :],
        send_sem=mask_send.at[3], recv_sem=mask_recv.at[3], device_id=sib, device_id_type=MESH)
    corner_send = pltpu.make_async_remote_copy(
        src_ref=corner, dst_ref=corner_a, send_sem=mask_send.at[4], recv_sem=mask_recv.at[4],
        device_id=prv, device_id_type=MESH)
    load_diagonal = pltpu.make_async_copy(up.at[pl.ds(0, H), 0], raw, load_sem.at[0])
    load = pltpu.make_async_copy(up, own, load_sem.at[1])
    load_mask = pltpu.make_async_copy(mask, mask_s, load_sem.at[2])
    load_keep = pltpu.make_async_copy(keep, keep_s, load_sem.at[3])

    barrier = pltpu.get_barrier_semaphore()
    pl.semaphore_signal(barrier, inc=1, device_id=nxt, device_id_type=MESH)
    pl.semaphore_signal(barrier, inc=1, device_id=sib, device_id_type=MESH)
    load_diagonal.start()
    load_mask.start()
    load_keep.start()
    load.start()
    pl.semaphore_wait(barrier, 2)
    mask_head.start()
    for j in range(H - 2):
        head(j).start()
    pl.semaphore_signal(ready, inc=1, device_id=prv, device_id_type=MESH)

    load_diagonal.wait()
    row_at = lax.broadcasted_iota(jnp.int32, (HALF, B), 0)
    lane_at = lax.broadcasted_iota(jnp.int32, (HALF, B), 1)
    corner[...] = jnp.zeros_like(corner)
    for j in range(H):
        x = raw[j]
        x = 0.5 * (x + x.T)
        low = x[HALF:]
        folded[j] = jnp.where(lane_at < row_at, pltpu.roll(low, HALF, 1), x[:HALF])
        corner[pl.ds(j, 1), :] = jnp.sum(jnp.where(lane_at == row_at + HALF, low, 0.0), axis=0, keepdims=True)
    fold_send.start()
    corner_send.start()
    for j in range(H - 2, H):
        head(j).start()

    zero_right = jnp.zeros((B, B), jnp.bfloat16)
    zero_left = jnp.zeros((HALF, B), jnp.bfloat16)

    def clear(pair, carry):
        for ref in (right_hi, right_lo):
            ref[pair, pl.ds(0, B), pl.ds(B, B)] = zero_right
            ref[pair, pl.ds((WINDOW - 1) * B, B), pl.ds(0, B)] = zero_right
        return carry

    lax.fori_loop(0, 2 * PAIRS, clear, 0)

    def clear_left(pair, carry):
        for base in (0, B):
            left[pair, pl.ds(base, HALF), pl.ds((WINDOW - 1) * B, B)] = zero_left
            left[pair, pl.ds(base + HALF, HALF), pl.ds(0, B)] = zero_left
        return carry

    lax.fori_loop(0, PAIRS, clear_left, 0)

    pl.semaphore_wait(ready, 1)
    mask_tail.start()
    for a in range(H):
        tail(a).start()
    load_mask.wait()
    load_keep.wait()
    load.wait()

    def place_right(pair, r, k, x):
        hi, lo = split(x)
        at = pair + (r + k) // 2
        rows = pl.ds((r + H - 2 * ((r + k) // 2)) * B, B)
        lanes = pl.ds(((r + k) % 2) * B, B)
        right_hi[at, rows, lanes] = hi
        right_lo[at, rows, lanes] = lo

    def place_right_t(pair, r, k, xt):
        hi, lo = split(xt)
        rows = pl.ds((r + k + H) * B, B)
        right_hi[pair, rows, pl.ds(r * B, B)] = hi
        right_lo[pair, rows, pl.ds(r * B, B)] = lo

    def my_half(x):
        return jnp.where(layer == 0, x[:HALF], x[HALF:])

    def place_left(pair, r, offset, xh):
        hi, lo = split(xh)
        lanes = pl.ds((r + offset + H) * B, B)
        left[pair, pl.ds(r * HALF, HALF), lanes] = hi
        left[pair, pl.ds(B + r * HALF, HALF), lanes] = lo

    def own_pair(pair, carry):
        for r in range(2):
            for k in range(H + 1):
                j = 2 * pair + r
                inside = first_row + j + k < total_rows
                if k > 0:
                    inside = inside & (mask_s[k, j] == 1)
                weight = jnp.where(inside, jnp.float32(1.0), jnp.float32(0.0))
                x = masked(weight, own[j, k])
                xt = x.T
                if k == 0:
                    x = 0.5 * (x + xt)
                place_right(pair, r, k, x)
                place_left(pair, r, k, my_half(x))
                if k > 0:
                    place_right_t(pair, r, k, xt)
                    own_row = pair + (r + k) // 2

                    @pl.when(own_row < PAIRS)
                    def _():
                        place_left(own_row, (r + k) % 2, -k, my_half(xt))

        return carry

    lax.fori_loop(0, PAIRS, own_pair, 0)

    def multiply(pair, d, lo_block, hi_block):
        return window_product(left, right_hi, right_lo, pair, d, lo_block, hi_block)

    def emit(pair, d, total, add):
        for r, s, m in places(d):
            i = 2 * pair + r
            piece = quarter(total, r, s) * keep_weight(keep_s, i, m, first_row, total_rows)
            if add:
                out[i, m] += piece
            else:
                out[i, m] = piece

    def own_low(d, first):
        def body(pair, carry):
            emit(pair, d, multiply(pair, d, 0, WINDOW - 2 * d), False)
            return carry

        lax.fori_loop(first, H // 2, body, 0)

    for d in range(H + 1):
        own_low(d, max(0, H // 2 - d))
    for pair in range(H // 2, PAIRS):
        for d in range(H + 1):
            c = pair + d
            if c < PAIRS:
                emit(pair, d, multiply(pair, d, 0, WINDOW - 2 * d), False)
            elif c < PAIRS + H // 2:
                emit(pair, d, multiply(pair, d, 0, 2 * (PAIRS + H // 2 - c)), False)

    for a in range(H):
        tail(a).wait_recv()
        tail_pass(a).start()
    for j in range(4):
        head(j).wait_recv()
        head_pass(j).start()
    fold_send.wait_recv()
    fold_pass.start()
    mask_tail.wait_recv()
    for a in range(H):
        tail_pass(a).wait_recv()
        j = -1 - a
        pair, r = j // 2, j % 2
        for k in range(a + 1, H + 1):
            present = (mask_b[pl.ds(k, 1), pl.ds(ROWS + j, 1)] == 1) & (part > 0)
            x = masked(jnp.where(present, jnp.float32(1.0), jnp.float32(0.0)), behind[a, k - a - 1])
            place_right(pair, r, k, x)
            place_left(pair + (r + k) // 2, (r + k) % 2, -k, my_half(x.T))
    for pair in range(H // 2):
        for d in range(H // 2 - pair):
            emit(pair, d, multiply(pair, d, 0, WINDOW - 2 * d), False)

    mask_head.wait_recv()
    corner_send.wait_recv()
    row_at = lax.broadcasted_iota(jnp.int32, (B, B), 0)
    lane_at = lax.broadcasted_iota(jnp.int32, (B, B), 1)
    top, leading = row_at < HALF, lane_at < HALF
    as_sent = (top & (~leading | (row_at <= lane_at))) | (~top & ~leading & (row_at > lane_at))
    on_corner = ~top & (row_at == lane_at)

    def unfold(j):
        x = folded_a[j]
        x = jnp.concatenate([x, pltpu.roll(x, HALF, 1)], axis=0)
        return jnp.where(on_corner, corner_a[pl.ds(j, 1), :], jnp.where(as_sent, x, x.T))

    def take(j):
        head(j).wait_recv()
        head_pass(j).start()

    def place_row(j):
        q, r = j // 2, j % 2
        head_pass(j).wait_recv()
        for k in range(H + 1):
            present = first_row + ROWS + j + k < total_rows
            weight = jnp.where(present, jnp.float32(1.0), jnp.float32(0.0))
            if k > 0:
                weight = jnp.where(mask_a[pl.ds(k, 1), pl.ds(j, 1)] == 1, weight, jnp.float32(0.0))
            x = masked(weight, ahead[j, k - 1] if k > 0 else unfold(j))
            place_right(PAIRS + q, r, k, x)
            if 0 < k < H - j:
                place_right_t(PAIRS + q, r, k, x.T)

    def add_terms(q):
        for pair in range(H // 2 + q, PAIRS):
            for c in range(PAIRS, PAIRS + q + H // 2 + 1):
                d = c - pair
                at = 2 * (PAIRS + q - (c - H // 2))
                first = c >= PAIRS + H // 2 and q == c - PAIRS - H // 2
                emit(pair, d, multiply(pair, d, at, at + 2), not first)

    take(4)
    take(5)
    fold_pass.wait_recv()
    place_row(0)
    place_row(1)
    add_terms(0)
    place_row(2)
    place_row(3)
    add_terms(1)
    place_row(4)
    place_row(5)

    for j in range(H):
        head(j).wait_send()
        tail(j).wait_send()
        head_pass(j).wait_send()
        tail_pass(j).wait_send()
    for copy in (mask_head, mask_tail, fold_send, fold_pass, corner_send):
        copy.wait_send()


def on_device(upper, block_mask, keep_mask):
    f32, bf16 = jnp.float32, jnp.bfloat16
    window = WINDOW * B
    spread = pl.pallas_call(
        kernel,
        out_shape=(
            pltpu.VMEM((ROWS, 2 * H + 1, HALF, B), f32),
            pltpu.VMEM((2 * PAIRS, window, 2 * B), bf16),
            pltpu.VMEM((2 * PAIRS, window, 2 * B), bf16),
            pltpu.VMEM((PAIRS, 2 * B, window), bf16),
        ),
        in_specs=[
            pl.BlockSpec(memory_space=pltpu.HBM),
            pl.BlockSpec(memory_space=pltpu.HBM),
            pl.BlockSpec(memory_space=pltpu.HBM),
        ],
        out_specs=[pl.BlockSpec(memory_space=pltpu.VMEM)] * 4,
        scratch_shapes=[
            pltpu.VMEM((ROWS, H + 1, B, B), f32),
            pltpu.VMEM((H, H, B, B), f32),
            pltpu.VMEM((H, H, B, B), f32),
            pltpu.VMEM((H + 1, ROWS), jnp.int32),
            pltpu.VMEM((H + 1, ROWS), jnp.int32),
            pltpu.SMEM((H + 1, ROWS), jnp.int32),
            pltpu.SMEM((ROWS, 2 * H + 1), jnp.int32),
            pltpu.VMEM((H, B, B), f32),
            pltpu.VMEM((H, HALF, B), f32),
            pltpu.VMEM((8, B), f32),
            pltpu.VMEM((H, HALF, B), f32),
            pltpu.VMEM((8, B), f32),
            pltpu.SemaphoreType.DMA((4,)),
            pltpu.SemaphoreType.DMA((2 * H,)),
            pltpu.SemaphoreType.DMA((2 * H,)),
            pltpu.SemaphoreType.DMA((2 * H,)),
            pltpu.SemaphoreType.DMA((2 * H,)),
            pltpu.SemaphoreType.DMA((5,)),
            pltpu.SemaphoreType.DMA((5,)),
            pltpu.SemaphoreType.REGULAR,
        ],
        compiler_params=pltpu.CompilerParams(
            collective_id=0, has_side_effects=True, vmem_limit_bytes=18 * 2**20
        ),
    )
    held = [pltpu.with_memory_space_constraint(x, pltpu.HBM) for x in (upper, block_mask.T, keep_mask)]
    parts = spread(*held)
    parts = [pltpu.with_memory_space_constraint(x, pltpu.VMEM) for x in parts]
    return pl.pallas_call(
        finish,
        out_shape=jax.ShapeDtypeStruct((ROWS, 2 * H + 1, HALF, B), f32),
        in_specs=[pl.BlockSpec(memory_space=pltpu.VMEM)] * 4 + [pl.BlockSpec(memory_space=pltpu.HBM)],
        out_specs=pl.BlockSpec(memory_space=pltpu.HBM),
        scratch_shapes=[
            pltpu.VMEM((2, 2 * H + 1, HALF, B), f32),
            pltpu.SMEM((ROWS, 2 * H + 1), jnp.int32),
            pltpu.SemaphoreType.DMA((PAIRS + 4,)),
        ],
        compiler_params=pltpu.CompilerParams(vmem_limit_bytes=8 * 2**20),
    )(*parts, held[2])


def solution(mesh):
    in_specs = (
        P(("row", "col"), None, None, None),
        P(("row", "col"), None),
        P(("row", "col"), None),
    )
    out_specs = P(("row", "col"), None, "layer", None)
    return jax.shard_map(
        on_device, mesh=mesh, in_specs=in_specs, out_specs=out_specs, check_vma=False
    )
```
